128 devices in a mesh: dp: 4 (over z), expert: 32 (over y, x, core).
Axes of the slice: x: 4, y: 4, z: 4, core: 2. Of those that a mesh axis runs over, the one named last changes fastest.
Arguments:
- tokens: bfloat16 [4096, 4096], P('expert'), may hold values from -6 to 6
- expert_ids: int32 [4096, 8], P('expert'), may hold values from 0 to 63, all different within a row; in each aligned block of 128 rows (0 to 127, 128 to 255, ...) at most 32 rows name the same one
- gate_prob: float32 [4096, 8], P('expert'), may hold values from 0.02 to 0.3
- gate_weight: bfloat16 [64, 4096, 1536], P('expert', None, 'dp'), may hold values from -0.09375 to 0.09375
- up_weight: bfloat16 [64, 4096, 1536], P('expert', None, 'dp'), may hold values from -0.09375 to 0.09375
- tangent: bfloat16 [64, 1536, 4096], P('expert', None, 'dp'), may hold values from -0.15625 to 0.15625
- curvature: float32 [4096], P('dp'), may hold values from 0.1 to 1.9
Outputs:
- hessian_product: bfloat16 [64, 1536, 4096], P('expert', None, 'dp')
- tangent_image: bfloat16 [4096, 4096], P('expert', 'dp')
The draws below stay inside these ranges and needn't reach their ends.
Inputs may be any that keep to these rules, and one draw needn't show every extreme that they name: `expert_ids`: each token names 8 different experts. Within each aligned block of 128 tokens no expert is named more than 32 times, and in every draw some expert is named exactly 32 times in some block.
All inputs are finite; a program needn't handle non-finite values.
Results may differ from the reference program's by a relative error of at most 0.007.
Values may be sent and summed in bfloat16 or wider, within the bound.
No kernel may reach another device: no remote copies, remote signals or barrier semaphores. Data moves between devices by JAX's collectives and lax.ppermute only.
A program may use at most 128 MiB of HBM per device.

```python
import math
from functools import partial
import jax
import jax.numpy as jnp
import numpy as np
from jax import lax

D = 4096
FF = 1536
TOP = 8
TOK_DEV = 128
EXPERTS = 64
CAP = 32
TOKENS = 4096
N_EXPERT = 32


def block_levels(rng, shape, pieces, low, top_value):
    factor_of = 1.0
    for dim, shards_of in pieces:
        steps = jax.random.uniform(jax.random.fold_in(jax.random.fold_in(rng, 6), dim), (shards_of,), jnp.float32, low / len(pieces), top_value / len(pieces))
        factor_of = factor_of * jnp.repeat(jnp.exp(steps), shape[dim] // shards_of).reshape((-1,) + (1,) * (len(shape) - 1 - dim))
    return factor_of


def routed_block(key, own, number, rows, number_of, top, most, lean):
    ranking = jax.random.permutation(key, number_of)
    crowded, ordinary = portions_of(number_of, rows * top, most, lean, True), portions_of(number_of, rows * top, most, lean, False)
    places = jnp.arange(number_of)

    def named(lengths, turn):
        used = int((lengths > 0).sum())
        fixed = max(1, used // 4)
        passed = fixed + (places - fixed + turn * (used - fixed)) % max(1, number_of - fixed)
        return jnp.zeros((number_of,), jnp.int32).at[ranking[jnp.where(places < fixed, places, passed)]].set(jnp.asarray(lengths, jnp.int32))

    lengths = jnp.where(number % 4 == 0, named(crowded, number // 4), named(ordinary, number - number // 4 - 1))
    mixed = jax.random.permutation(jax.random.fold_in(own, 3), number_of)
    giver, taker = mixed[0:number_of // 2 * 2:2], mixed[1:number_of // 2 * 2:2]
    slack = jnp.minimum(lengths[giver] - 1, most - lengths[taker]) // 2
    slack = jnp.where((giver == ranking[0]) | (taker == ranking[0]) | (lengths[taker] == 0), 0, jnp.maximum(slack, 0))
    passed = jax.random.randint(jax.random.fold_in(own, 4), (number_of // 2,), 0, 1 << 20) % (slack + 1)
    lengths = lengths.at[giver].add(-passed).at[taker].add(passed)
    members = jnp.searchsorted(jnp.cumsum(lengths), jnp.arange(rows * top), side="right").astype(jnp.int32)
    listing = members.reshape(top, rows).T
    listing = listing[jax.random.permutation(jax.random.fold_in(own, 1), rows)]
    turn = jax.random.randint(jax.random.fold_in(own, 2), (rows, 1), 0, top)
    return jnp.take_along_axis(listing, (jnp.arange(top)[None, :] + turn) % top, axis=1)


def portions_of(amount, total, reach, skew, full):
    loads = [(1 << 20) // math.isqrt(standing ** skew) + 1 for standing in range(1, amount + 1)]
    largest = reach if full else min(reach, max(-(-total // amount), total * loads[0] // sum(loads)))
    least = 1 if total - largest >= amount - 1 else 0
    given, spare = [largest] + [least] * (amount - 1), total - largest - least * (amount - 1)
    while spare > 0:
        free = [i for i in range(1, amount) if given[i] < largest] or [i for i in range(1, amount) if given[i] < reach]
        whole, budget = sum([loads[i] for i in free]), spare
        for i in free:
            more = min(reach - given[i], max(1, budget * loads[i] // whole), spare)
            given[i] = given[i] + more
            spare = spare - more
    return np.array(given)


def normal_values(own_key, shape, width, reach, cuts=(), held_as=jnp.bfloat16):
    drawn = width * jax.random.normal(own_key, shape, jnp.float32)
    if cuts:
        drawn = drawn * block_levels(own_key, shape, cuts, -0.22, 0.18)
    return jnp.clip(drawn, -reach, reach).astype(held_as)


def setup_inputs(seed: int = 0) -> dict:
    key_list = jax.random.split(jax.random.key(seed), 8)
    tokens = normal_values(key_list[0], (TOKENS, D), 1.0, 6.0, ((0, 32),))
    expert_ids_keys = jax.random.split(jax.random.fold_in(key_list[1], 1), TOKENS // TOK_DEV)
    expert_ids_turns = jax.random.permutation(jax.random.fold_in(key_list[1], 3), TOKENS // TOK_DEV)
    expert_ids = jax.vmap(lambda own, number: routed_block(jax.random.fold_in(key_list[1], 2), own, number, TOK_DEV, EXPERTS, TOP, CAP, 2))(expert_ids_keys, expert_ids_turns).reshape((TOKENS, TOP))
    gate_prob = jnp.clip(0.02 + 0.28 * jax.random.uniform(key_list[2], (TOKENS, TOP), jnp.float32) ** block_levels(key_list[2], (TOKENS, TOP), ((0, 32),), -0.2, 0.2), 0.02, 0.3)
    gate_weight = normal_values(key_list[3], (EXPERTS, D, FF), D ** -0.5, 0.09375, ((0, 32), (2, 4)))
    up_weight = normal_values(key_list[4], (EXPERTS, D, FF), D ** -0.5, 0.09375, ((0, 32), (2, 4)))
    tangent = normal_values(key_list[5], (EXPERTS, FF, D), FF ** -0.5, 0.15625, ((0, 32), (2, 4)))
    curvature = jnp.clip(1.0 + 0.18 * jax.random.normal(key_list[6], (D,), jnp.float32), 0.1, 1.9)
    return dict(tokens=tokens, expert_ids=expert_ids, gate_prob=gate_prob, gate_weight=gate_weight, up_weight=up_weight, tangent=tangent, curvature=curvature)


def slot_of_rows(flat_ids, expert_total, capacity):
    onehot = (flat_ids[:, None] == jnp.arange(expert_total, dtype=jnp.int32)[None, :]).astype(jnp.int32)
    earlier = jnp.cumsum(onehot, axis=0, dtype=jnp.int32) - onehot
    position = jnp.sum(earlier * onehot, axis=1, dtype=jnp.int32)
    return flat_ids * capacity + position


def row_of_slots(slots, expert_total, capacity):
    row_total = slots.shape[0]
    empty_rows = jnp.full((expert_total * capacity,), row_total, jnp.int32)
    return empty_rows.at[slots].set(jnp.arange(row_total, dtype=jnp.int32))


def reference(tokens, expert_ids, gate_prob, gate_weight, up_weight, tangent, curvature):
    block_rows = TOK_DEV * TOP
    flat_ids = expert_ids.reshape(N_EXPERT, block_rows)
    slots = jax.vmap(partial(slot_of_rows, expert_total=EXPERTS, capacity=CAP))(flat_ids)
    owners = jax.vmap(partial(row_of_slots, expert_total=EXPERTS, capacity=CAP))(slots)
    offsets = (jnp.arange(N_EXPERT, dtype=jnp.int32) * block_rows)[:, None]
    global_rows = jnp.where(owners < block_rows, owners + offsets, TOKENS * TOP).astype(jnp.int32)
    per_expert = global_rows.reshape(N_EXPERT, EXPERTS, CAP).transpose(1, 0, 2).reshape(EXPERTS, N_EXPERT * CAP)
    padded_tokens = jnp.concatenate([tokens, jnp.zeros((1, D), tokens.dtype)], axis=0)
    padded_prob = jnp.concatenate([gate_prob.reshape(TOKENS * TOP), jnp.zeros((1,), jnp.float32)], axis=0)

    def forward_expert(running, inputs):
        rows_here, gate_mat, up_mat, tangent_mat = inputs
        token_index = rows_here // TOP
        expert_in = padded_tokens[token_index]
        gate_pre = jnp.dot(expert_in, gate_mat, preferred_element_type=jnp.float32)
        up_pre = jnp.dot(expert_in, up_mat, preferred_element_type=jnp.float32)
        hidden = (jax.nn.silu(gate_pre) * up_pre).astype(jnp.bfloat16)
        expert_out = jnp.dot(hidden, tangent_mat, preferred_element_type=jnp.float32).astype(jnp.bfloat16)
        weight_here = padded_prob[rows_here]
        running = running.at[token_index].add(weight_here[:, None] * expert_out.astype(jnp.float32))
        return running, hidden

    start_sum = jnp.zeros((TOKENS + 1, D), jnp.float32)
    running, hidden_all = lax.scan(forward_expert, start_sum, (per_expert, gate_weight, up_weight, tangent))
    combined = running[:TOKENS]
    tangent_image = combined.astype(jnp.bfloat16)
    weighted = curvature[None, :] * combined
    padded_weighted = jnp.concatenate([weighted, jnp.zeros((1, D), jnp.float32)], axis=0)

    def backward_expert(inputs):
        rows_here, hidden = inputs
        scaled = (padded_prob[rows_here][:, None] * padded_weighted[rows_here // TOP]).astype(jnp.bfloat16)
        return jnp.dot(hidden.T, scaled, preferred_element_type=jnp.float32).astype(jnp.bfloat16)

    hessian_product = lax.map(backward_expert, (per_expert, hidden_all))
    return hessian_product, tangent_image
```

```python
import functools

import jax
import jax.numpy as jnp
from jax import lax
from jax.experimental import pallas as pl
from jax.experimental.pallas import tpu as pltpu
from jax.sharding import PartitionSpec as P

BF = jnp.bfloat16
F32 = jnp.float32
SIDE = 4
BLK = 128
CAP = 32
SLOTS = 4 * CAP
META = 128
TOP = 8
PARTS = 4
LIMIT = 48 << 20


def params(*semantics):
    return pltpu.CompilerParams(
        dimension_semantics=semantics, vmem_limit_bytes=LIMIT
    )


def cost(flops, nbytes):
    return pl.CostEstimate(flops=flops, bytes_accessed=nbytes, transcendentals=0)


def spot(y, x, core):
    return ((y % SIDE) * SIDE + x % SIDE) * 2 + core


def pairs(stage, step):
    out = []
    for y in range(SIDE):
        for x in range(SIDE):
            for core in range(2):
                along_x = (core == 0) == (stage == "a")
                to = spot(y, x + step, core) if along_x else spot(y + step, x, core)
                out.append((spot(y, x, core), to))
    return out


def move(value, stage, step):
    return lax.ppermute(value, "expert", pairs(stage, step))


def swap(value):
    return lax.ppermute(value, "expert", [(i, i ^ 1) for i in range(2 * SIDE * SIDE)])


def move_z(value, step):
    return lax.ppermute(value, "dp", [(i, (i + step) % PARTS) for i in range(PARTS)])


def dot(a, b, dims=((1,), (0,))):
    return lax.dot_general(a, b, (dims, ((), ())), preferred_element_type=F32)


def select_kernel(counts, experts, *refs):
    n = len(counts)
    blocks, metas = refs[:n], refs[n : 2 * n]
    mine, theirs, weight = refs[2 * n : 2 * n + 3]
    picks = refs[2 * n + 3]
    where = [(i, j) for i in range(n) for j in range(counts[i])]

    @pl.when(pl.program_id(0) == 0)
    def _():
        slot = lax.broadcasted_iota(jnp.int32, (BLK, SLOTS), 1)
        group = slot // CAP
        expert = jnp.where(
            group < 2, experts[0] + group, experts[1] + group - 2
        ).astype(F32)
        place = (slot % CAP).astype(F32)
        row = lax.broadcasted_iota(jnp.int32, (BLK, BLK), 0)
        column = lax.broadcasted_iota(jnp.int32, (BLK, BLK), 1)
        earlier = (column < row).astype(F32).astype(BF)
        for b, (i, j) in enumerate(where):
            meta = metas[i][j].astype(F32)
            named = jnp.zeros((BLK, SLOTS), F32)
            prob = jnp.zeros((BLK, SLOTS), F32)
            for k in range(TOP):
                hit = meta[:, k : k + 1] == expert
                named = jnp.where(hit, 1.0, named)
                value = meta[:, TOP + k : TOP + k + 1] + meta[:, 2 * TOP + k : 2 * TOP + k + 1]
                prob = jnp.where(hit, value, prob)
            position = dot(earlier, named.astype(BF))
            chosen = (named > 0.5) & (position == place)
            picks[b] = jnp.where(chosen, 1.0, 0.0).astype(BF)
            kept = jnp.where(chosen, prob, 0.0)
            high = kept.astype(BF)
            weight[b, 0] = high
            weight[b, 1] = (kept - high.astype(F32)).astype(BF)

    for b, (i, j) in enumerate(where):
        rows = dot(picks[b], blocks[i][j], ((0,), (0,))).astype(BF)
        at = pl.ds(b * CAP, CAP)
        mine[0, at, :] = rows[0:CAP]
        mine[1, at, :] = rows[CAP : 2 * CAP]
        theirs[0, at, :] = rows[2 * CAP : 3 * CAP]
        theirs[1, at, :] = rows[3 * CAP :]


def select(experts, blocks, width):
    counts = [v.shape[0] for v in blocks]
    four = sum(counts)
    tile = 1024
    grid = (width // tile,)
    rows = jax.ShapeDtypeStruct((2, four * CAP, width), BF)
    weight = jax.ShapeDtypeStruct((four, 2, BLK, SLOTS), BF)
    row_spec = pl.BlockSpec((2, four * CAP, tile), lambda j, s: (0, 0, j))
    return pl.pallas_call(
        functools.partial(select_kernel, counts),
        out_shape=(rows, rows, weight),
        grid_spec=pltpu.PrefetchScalarGridSpec(
            num_scalar_prefetch=1,
            grid=grid,
            in_specs=[pl.BlockSpec((c, BLK, tile), lambda j, s: (0, 0, j)) for c in counts]
            + [
                pl.BlockSpec((c, BLK, META), lambda j, s: (0, 0, width // META))
                for c in counts
            ],
            out_specs=(
                row_spec,
                row_spec,
                pl.BlockSpec((four, 2, BLK, SLOTS), lambda j, s: (0, 0, 0, 0)),
            ),
            scratch_shapes=[pltpu.VMEM((four, BLK, SLOTS), BF)],
        ),
        compiler_params=params("arbitrary"),
        cost_estimate=cost(2 * four * BLK * SLOTS * width, 4 * four * BLK * width),
        name="select_rows",
    )(experts, *blocks, *blocks)


def hidden_kernel(xa, xb, gate, up, out, gate_acc, up_acc):
    k = pl.program_id(1)

    @pl.when(k == 0)
    def _():
        gate_acc[...] = jnp.zeros_like(gate_acc)
        up_acc[...] = jnp.zeros_like(up_acc)

    x = jnp.concatenate([xa[0], xb[0]], axis=0)
    gate_acc[...] += dot(x, gate[0])
    up_acc[...] += dot(x, up[0])

    @pl.when(k == pl.num_programs(1) - 1)
    def _():
        g = gate_acc[...]
        out[0] = (g / (1.0 + jnp.exp(-g)) * up_acc[...]).astype(BF)


def hidden_share(xa, xb, gate, up):
    experts, rows, width = xa.shape
    share = gate.shape[2]
    tile = 1024
    x_spec = pl.BlockSpec((1, rows, tile), lambda e, k: (e, 0, k))
    w_spec = pl.BlockSpec((1, tile, share), lambda e, k: (e, k, 0))
    return pl.pallas_call(
        hidden_kernel,
        out_shape=jax.ShapeDtypeStruct((experts, 2 * rows, share), BF),
        grid=(experts, width // tile),
        in_specs=[x_spec, x_spec, w_spec, w_spec],
        out_specs=pl.BlockSpec((1, 2 * rows, share), lambda e, k: (e, 0, 0)),
        scratch_shapes=[pltpu.VMEM((2 * rows, share), F32)] * 2,
        compiler_params=params("arbitrary", "arbitrary"),
        cost_estimate=cost(
            8 * experts * rows * width * share, 4 * experts * width * (share + rows)
        ),
        name="hidden_share",
    )(xa, xb, gate, up)


SOURCES = (0, PARTS - 1, 1, 2)


def source_of(k, z):
    shift = jnp.where(k == 0, 0, jnp.where(k == 1, PARTS - 1, k - 1))
    return lax.rem(z + shift, PARTS)


def out_kernel(z, own, below, above, far0, far1, tangent, out_a, out_b, held, acc):
    e, k = pl.program_id(0), pl.program_id(1)

    @pl.when(k == 0)
    def _():
        held[0, 0] = own[0]

    @pl.when(k == 1)
    def _():
        held[0, 0] = below[0]

    @pl.when(k == 2)
    def _():
        held[0, 0] = above[0]

    @pl.when((k == 3) & (e == 0))
    def _():
        held[0, 0] = far0[0]

    @pl.when((k == 3) & (e == 1))
    def _():
        held[0, 0] = far1[0]

    product = dot(held[0, 0], tangent[0])

    @pl.when(k == 0)
    def _():
        acc[...] = product

    @pl.when(k > 0)
    def _():
        acc[...] += product

    @pl.when(k == pl.num_programs(1) - 1)
    def _():
        half = acc.shape[0] // 2
        out_a[0] = acc[:half].astype(BF)
        out_b[0] = acc[half:].astype(BF)


def expert_out(z, own, below, above, far0, far1, tangent):
    experts, rows, share = own.shape
    width = tangent.shape[2]
    h_spec = pl.BlockSpec((1, rows, share), lambda e, k, s: (e, 0, 0))
    f_spec = pl.BlockSpec((1, rows, share), lambda e, k, s: (0, 0, 0))
    o_spec = pl.BlockSpec((1, rows // 2, width), lambda e, k, s: (e, 0, 0))
    half = jax.ShapeDtypeStruct((experts, rows // 2, width), BF)
    return pl.pallas_call(
        out_kernel,
        out_shape=(half, half, jax.ShapeDtypeStruct((PARTS, experts, rows, share), BF)),
        grid_spec=pltpu.PrefetchScalarGridSpec(
            num_scalar_prefetch=1,
            grid=(experts, PARTS),
            in_specs=[h_spec] * 3
            + [f_spec] * 2
            + [pl.BlockSpec((1, share, width), lambda e, k, s: (e, source_of(k, s[0]), 0))],
            out_specs=(
                o_spec,
                o_spec,
                pl.BlockSpec((1, 1, rows, share), lambda e, k, s: (k, e, 0, 0)),
            ),
            scratch_shapes=[pltpu.VMEM((rows, width), F32)],
        ),
        compiler_params=params("arbitrary", "arbitrary"),
        cost_estimate=cost(
            2 * experts * rows * share * PARTS * width,
            2 * experts * (share * PARTS * width + 2 * rows * share * PARTS + rows * width),
        ),
        name="expert_out",
    )(z, own, below, above, far0, far1, tangent)


def combine_kernel(mine, theirs, weight, first, second):
    for b in range(4):
        at = pl.ds(b * CAP, CAP)
        rows = jnp.concatenate(
            [mine[0, at, :], mine[1, at, :], theirs[0, at, :], theirs[1, at, :]], axis=0
        )
        part = (dot(weight[b, 0], rows) + dot(weight[b, 1], rows)).astype(BF)
        if b < 2:
            first[b] = part
        else:
            second[b - 2] = part


def combine(mine, theirs, weight):
    width = mine.shape[2]
    tile = 512
    in_spec = pl.BlockSpec((2, 4 * CAP, tile), lambda j: (0, 0, j))
    out_spec = pl.BlockSpec((2, BLK, tile), lambda j: (0, 0, j))
    shape = jax.ShapeDtypeStruct((2, BLK, width), BF)
    return pl.pallas_call(
        combine_kernel,
        out_shape=(shape, shape),
        grid=(width // tile,),
        in_specs=[
            in_spec,
            in_spec,
            pl.BlockSpec((4, 2, BLK, SLOTS), lambda j: (0, 0, 0, 0)),
        ],
        out_specs=(out_spec, out_spec),
        compiler_params=params("arbitrary"),
        cost_estimate=cost(16 * BLK * SLOTS * width, 16 * BLK * width),
        name="combine_rows",
    )(mine, theirs, weight)


def scaled_kernel(first, second, weight, mine, theirs):
    for b in range(4):
        block = first[b] if b < 2 else second[b - 2]
        rows = (
            dot(weight[b, 0], block, ((0,), (0,))) + dot(weight[b, 1], block, ((0,), (0,)))
        ).astype(BF)
        at = pl.ds(b * CAP, CAP)
        mine[0, at, :] = rows[0:CAP]
        mine[1, at, :] = rows[CAP : 2 * CAP]
        theirs[0, at, :] = rows[2 * CAP : 3 * CAP]
        theirs[1, at, :] = rows[3 * CAP :]


def scaled_rows(first, fi, second, si, weight):
    width = first.shape[2]
    tile = 512
    out_spec = pl.BlockSpec((2, 4 * CAP, tile), lambda j: (0, 0, j))
    shape = jax.ShapeDtypeStruct((2, 4 * CAP, width), BF)
    return pl.pallas_call(
        scaled_kernel,
        out_shape=(shape, shape),
        grid=(width // tile,),
        in_specs=[
            pl.BlockSpec((2, BLK, tile), lambda j: (fi, 0, j)),
            pl.BlockSpec((2, BLK, tile), lambda j: (si, 0, j)),
            pl.BlockSpec((4, 2, BLK, SLOTS), lambda j: (0, 0, 0, 0)),
        ],
        out_specs=(out_spec, out_spec),
        compiler_params=params("arbitrary"),
        cost_estimate=cost(16 * BLK * SLOTS * width, 16 * BLK * width),
        name="scaled_rows",
    )(first, second, weight)


def hessian_kernel(z, *refs):
    n = (len(refs) - 1) // 3
    held, mine, theirs, out = refs[:n], refs[n : 2 * n], refs[2 * n : 3 * n], refs[-1]
    total = None
    for g in range(n):
        scaled = jnp.concatenate([mine[g][0], theirs[g][0]], axis=0)
        part = dot(held[g][0, 0], scaled, ((0,), (0,)))
        total = part if total is None else total + part
    out[0] = total.astype(BF)


def hessian(z, held, mine, theirs):
    _, experts, rows, share = held[0].shape
    width = mine[0].shape[2]
    n = len(held)
    return pl.pallas_call(
        hessian_kernel,
        out_shape=jax.ShapeDtypeStruct((experts, PARTS * share, width), BF),
        grid_spec=pltpu.PrefetchScalarGridSpec(
            num_scalar_prefetch=1,
            grid=(experts, PARTS),
            in_specs=[pl.BlockSpec((1, 1, rows, share), lambda e, k, s: (k, e, 0, 0))] * n
            + [pl.BlockSpec((1, rows // 2, width), lambda e, k, s: (e, 0, 0))] * (2 * n),
            out_specs=pl.BlockSpec(
                (1, share, width), lambda e, k, s: (e, source_of(k, s[0]), 0)
            ),
        ),
        compiler_params=params("arbitrary", "arbitrary"),
        cost_estimate=cost(
            2 * n * experts * rows * share * PARTS * width,
            2 * experts * (share * PARTS * width + n * rows * (share * PARTS + width)),
        ),
        name="hessian",
    )(z, *held, *mine, *theirs)


def per_device(tokens, expert_ids, gate_prob, gate_weight, up_weight, tangent, curvature):
    width = tokens.shape[1]
    me = lax.axis_index("expert").astype(jnp.int32)
    z = lax.axis_index("dp").astype(jnp.int32)[None]
    partner = me + 1 - 2 * (me % 2)
    experts = jnp.stack([2 * me, 2 * partner])

    high = lax.reduce_precision(gate_prob, 8, 7)
    rest = gate_prob - high
    meta = jnp.concatenate(
        [expert_ids.astype(BF), high.astype(BF), rest.astype(BF)], axis=1
    )
    meta = jnp.pad(meta, ((0, 0), (0, META - meta.shape[1])))
    block = jnp.concatenate([tokens, meta], axis=1)

    half = BLK // 2
    low = move(block, "a", 1)
    upper = move(block, "a", -1)
    far_low = move(low[:half], "a", 1)
    far_high = move(upper[half:], "a", -1)
    pair_p = jnp.stack([block, low])
    pair_q = jnp.stack([upper, jnp.concatenate([far_low, far_high], axis=0)])
    p_low, p_up = move(pair_p, "b", 1), move(pair_p, "b", -1)
    q_low, q_up = move(pair_q, "b", 1), move(pair_q, "b", -1)
    far = [
        move(p_low[:1], "b", 1),
        move(p_up[1:], "b", -1),
        move(q_low[:1], "b", 1),
        move(q_up[1:], "b", -1),
    ]
    groups = [[pair_p, pair_q], [p_low, p_up], [q_low, q_up], far]

    weights, helds, parts = [], [], []
    for blocks in groups:
        mine, theirs, weight = select(experts, blocks, width)
        other = swap(theirs)
        own = hidden_share(mine, other, gate_weight, up_weight)
        below, above = move_z(own, 1), move_z(own, -1)
        far0, far1 = move_z(below[:1], 1), move_z(above[1:], -1)
        out_a, out_b, held = expert_out(z, own, below, above, far0, far1, tangent)
        parts.append(combine(out_a, swap(out_b), weight))
        weights.append(weight)
        helds.append(held)

    p_parts = [parts[0][0], move(parts[1][0], "b", -1), move(parts[1][1], "b", 1)]
    q_parts = [parts[0][1], move(parts[2][0], "b", -1), move(parts[2][1], "b", 1)]
    far_parts = move(jnp.concatenate(parts[3], axis=0), "b", 2)
    p_sum = sum(v.astype(F32) for v in p_parts) + far_parts[:2].astype(F32)
    q_sum = sum(v.astype(F32) for v in q_parts) + far_parts[2:].astype(F32)
    from_up = move(p_sum[1].astype(BF), "a", -1)
    from_low = move(q_sum[0].astype(BF), "a", 1)
    from_far = move(q_sum[1].astype(BF), "a", 2)
    combined = (
        p_sum[0] + from_up.astype(F32) + from_low.astype(F32) + from_far.astype(F32)
    )
    tangent_image = combined.astype(BF)
    weighted = (curvature[None, :] * combined).astype(BF)

    row = jnp.stack(
        [
            weighted,
            move(weighted, "a", 1),
            move(weighted, "a", -1),
            move(weighted, "a", 2),
        ]
    )
    r_low, r_up = move(row, "b", 1), move(row, "b", -1)
    r_far0, r_far1 = None, None
    r_far0 = move(r_low[:2], "b", 1)
    r_far1 = move(r_up[2:], "b", -1)
    sources = [(row, 0, row, 1), (r_low, 0, r_up, 0), (r_low, 1, r_up, 1), (r_far0, 0, r_far1, 0)]
    mines, others = [], []
    for (first, fi, second, si), weight in zip(sources, weights):
        mine, theirs = scaled_rows(first, fi, second, si, weight)
        mines.append(mine)
        others.append(swap(theirs))
    return hessian(z, helds, mines, others), tangent_image


def solution(mesh):
    placed = (
        P("expert", None),
        P("expert", None),
        P("expert", None),
        P("expert", None, "dp"),
        P("expert", None, "dp"),
        P("expert", None, "dp"),
        P("dp"),
    )
    return jax.shard_map(
        per_device,
        mesh=mesh,
        in_specs=placed,
        out_specs=(P("expert", None, "dp"), P("expert", "dp")),
        check_vma=False,
    )
```

```python
import functools

import jax
import jax.numpy as jnp
from jax import lax
from jax.experimental import pallas as pl
from jax.experimental.pallas import tpu as pltpu
from jax.sharding import PartitionSpec as P

BF = jnp.bfloat16
F32 = jnp.float32
SIDE = 4
BLK = 128
CAP = 32
SLOTS = 4 * CAP
META = 128
TOP = 8
PARTS = 4
LIMIT = 20 << 20


def params():
    return pltpu.CompilerParams(vmem_limit_bytes=LIMIT)


VMEM = pl.BlockSpec(memory_space=pltpu.VMEM)
SMEM = pl.BlockSpec(memory_space=pltpu.SMEM)


def cost(flops, nbytes):
    return pl.CostEstimate(flops=1, bytes_accessed=1, transcendentals=0)


def spot(y, x, core):
    return ((y % SIDE) * SIDE + x % SIDE) * 2 + core


def pairs(stage, step):
    out = []
    for y in range(SIDE):
        for x in range(SIDE):
            for core in range(2):
                along_x = (core == 0) == (stage == "a")
                to = spot(y, x + step, core) if along_x else spot(y + step, x, core)
                out.append((spot(y, x, core), to))
    return out


def move(value, stage, step):
    return lax.ppermute(value, "expert", pairs(stage, step))


def swap(value):
    return lax.ppermute(value, "expert", [(i, i ^ 1) for i in range(2 * SIDE * SIDE)])


def move_z(value, step):
    return lax.ppermute(value, "dp", [(i, (i + step) % PARTS) for i in range(PARTS)])


def after(value, *earlier):
    return lax.optimization_barrier((value, *earlier))[0]


def dot(a, b, dims=((1,), (0,))):
    return lax.dot_general(a, b, (dims, ((), ())), preferred_element_type=F32)


def select_kernel(experts, *refs):
    given = refs[:-3]
    mine, theirs, weight = refs[-3:]
    blocks = [v.at[i] for v in given for i in range(v.shape[0])]
    n = len(blocks)
    width = mine.shape[2]
    slot = lax.broadcasted_iota(jnp.int32, (BLK, SLOTS), 1)
    group = slot // CAP
    expert = jnp.where(group < 2, experts[0] + group, experts[1] + group - 2).astype(F32)
    place = (slot % CAP).astype(F32)
    row = lax.broadcasted_iota(jnp.int32, (BLK, BLK), 0)
    column = lax.broadcasted_iota(jnp.int32, (BLK, BLK), 1)
    earlier = (column < row).astype(F32).astype(BF)
    for b in range(n):
        meta = blocks[b][:, width:].astype(F32)
        named = jnp.zeros((BLK, SLOTS), F32)
        prob = jnp.zeros((BLK, SLOTS), F32)
        for k in range(TOP):
            hit = meta[:, k : k + 1] == expert
            named = jnp.where(hit, 1.0, named)
            value = meta[:, TOP + k : TOP + k + 1] + meta[:, 2 * TOP + k : 2 * TOP + k + 1]
            prob = jnp.where(hit, value, prob)
        position = dot(earlier, named.astype(BF))
        chosen = (named > 0.5) & (position == place)
        pick = jnp.where(chosen, 1.0, 0.0).astype(BF)
        kept = jnp.where(chosen, prob, 0.0)
        high = kept.astype(BF)
        weight[b, 0] = high
        weight[b, 1] = (kept - high.astype(F32)).astype(BF)
        rows = dot(pick, blocks[b][:, :width], ((0,), (0,))).astype(BF)
        at = pl.ds(b * CAP, CAP)
        mine[0, at, :] = rows[0:CAP]
        mine[1, at, :] = rows[CAP : 2 * CAP]
        theirs[0, at, :] = rows[2 * CAP : 3 * CAP]
        theirs[1, at, :] = rows[3 * CAP :]


def select(experts, blocks, width):
    n = sum(v.shape[0] for v in blocks)
    rows = jax.ShapeDtypeStruct((2, n * CAP, width), BF)
    weight = jax.ShapeDtypeStruct((n, 2, BLK, SLOTS), BF)
    return pl.pallas_call(
        select_kernel,
        out_shape=(rows, rows, weight),
        in_specs=[SMEM] + [VMEM] * len(blocks),
        out_specs=(VMEM,) * 3,
        compiler_params=params(),
        cost_estimate=cost(2 * n * BLK * SLOTS * width, 4 * n * BLK * width),
        name="select_rows",
    )(experts, *blocks)


def hidden_kernel(xa, xb, gate, up, out):
    share = out.shape[2]
    whole = share // 256 * 256
    for e in range(out.shape[0]):
        x = jnp.concatenate([xa[e], xb[e]], axis=0)
        tail = jnp.concatenate([gate[e, :, whole:], up[e, :, whole:]], axis=1)
        both = dot(x, tail)
        part = share - whole
        g = jnp.concatenate([dot(x, gate[e, :, :whole]), both[:, :part]], axis=1)
        u = jnp.concatenate([dot(x, up[e, :, :whole]), both[:, part:]], axis=1)
        out[e] = (g / (1.0 + jnp.exp(-g)) * u).astype(BF)


def hidden_share(xa, xb, gate, up):
    experts, rows, width = xa.shape
    share = gate.shape[2]
    return pl.pallas_call(
        hidden_kernel,
        out_shape=jax.ShapeDtypeStruct((experts, 2 * rows, share), BF),
        in_specs=[VMEM] * 4,
        out_specs=VMEM,
        compiler_params=params(),
        cost_estimate=cost(
            8 * experts * rows * width * share, 4 * experts * width * (share + rows)
        ),
        name="hidden_share",
    )(xa, xb, gate, up)


def expert_out_kernel(n, *refs):
    helds, refs = refs[:n], refs[n:]
    if len(refs) > 3:
        z, own, below, above, far0, far1, tangent, out_a, out_b, ring = refs
        me = z[0]
        ring[me] = own[...]
        ring[lax.rem(me + PARTS - 1, PARTS)] = below[...]
        ring[lax.rem(me + 1, PARTS)] = above[...]
        far = lax.rem(me + 2, PARTS)
        ring[far, 0] = far0[0]
        ring[far, 1] = far1[0]
        helds = (*helds, ring)
    else:
        tangent, out_a, out_b = refs
    for g, held in enumerate(helds):
        half = held.shape[2] // 2
        at = pl.ds(g * half, half)
        for e in range(tangent.shape[0]):
            x = jnp.concatenate([held[k, e] for k in range(PARTS)], axis=1)
            rows = dot(x, tangent[e])
            out_a[e, at, :] = rows[:half].astype(BF)
            out_b[e, at, :] = rows[half:].astype(BF)


def expert_out(tangent, helds, ring=()):
    experts, units, width = tangent.shape
    half = sum(v.shape[2] for v in helds) // 2
    outs = []
    if ring:
        rows = ring[1].shape[1]
        half += rows // 2
        outs = [jax.ShapeDtypeStruct((PARTS, experts, rows, units // PARTS), BF)]
    shape = jax.ShapeDtypeStruct((experts, half, width), BF)
    return pl.pallas_call(
        functools.partial(expert_out_kernel, len(helds)),
        out_shape=[shape, shape, *outs],
        in_specs=[VMEM] * len(helds) + ([SMEM] + [VMEM] * 5 if ring else []) + [VMEM],
        out_specs=[VMEM] * (2 + len(outs)),
        compiler_params=params(),
        cost_estimate=cost(4 * experts * half * units * width, 2 * experts * units * width),
        name="expert_out",
    )(*helds, *ring, tangent)


def combine_kernel(places, n, mine, theirs, *refs):
    weights, outs = refs[:n], refs[n:]
    for b, (i, j) in enumerate(places):
        at = pl.ds(b * CAP, CAP)
        rows = jnp.concatenate(
            [mine[0, at, :], mine[1, at, :], theirs[0, at, :], theirs[1, at, :]], axis=0
        )
        weight = weights[b // 4]
        outs[i][j] = (dot(weight[b % 4, 0], rows) + dot(weight[b % 4, 1], rows)).astype(BF)


def combine(places, mine, theirs, weights):
    width = mine.shape[2]
    counts = [sum(p[0] == i for p in places) for i in range(1 + max(p[0] for p in places))]
    return pl.pallas_call(
        functools.partial(combine_kernel, places, len(weights)),
        out_shape=[jax.ShapeDtypeStruct((c, BLK, width), BF) for c in counts],
        in_specs=[VMEM] * (2 + len(weights)),
        out_specs=[VMEM] * len(counts),
        compiler_params=params(),
        cost_estimate=cost(4 * len(places) * BLK * SLOTS * width, 4 * len(places) * BLK * width),
        name="combine_rows",
    )(mine, theirs, *weights)


def scaled_kernel(*refs):
    *blocks, weight, mine, theirs = refs
    for b in range(weight.shape[0]):
        block = blocks[b // 2][b % 2]
        rows = (
            dot(weight[b, 0], block, ((0,), (0,))) + dot(weight[b, 1], block, ((0,), (0,)))
        ).astype(BF)
        at = pl.ds(b * CAP, CAP)
        mine[0, at, :] = rows[0:CAP]
        mine[1, at, :] = rows[CAP : 2 * CAP]
        theirs[0, at, :] = rows[2 * CAP : 3 * CAP]
        theirs[1, at, :] = rows[3 * CAP :]


def scaled_rows(sources, weight):
    width = sources[0][0].shape[2]
    n = weight.shape[0]
    tile = 512
    out_spec = pl.BlockSpec((2, n * CAP, tile), lambda j: (0, 0, j))
    shape = jax.ShapeDtypeStruct((2, n * CAP, width), BF)
    return pl.pallas_call(
        scaled_kernel,
        out_shape=(shape, shape),
        grid=(width // tile,),
        in_specs=[
            pl.BlockSpec((2, BLK, tile), functools.partial(lambda i, j: (i, 0, j), i))
            for _, i in sources
        ]
        + [pl.BlockSpec(weight.shape, lambda j: (0, 0, 0, 0))],
        out_specs=(out_spec, out_spec),
        compiler_params=params(),
        cost_estimate=cost(4 * n * BLK * SLOTS * width, 4 * n * BLK * width),
        name="scaled_rows",
    )(*[v for v, _ in sources], weight)


def hessian_kernel(*refs):
    n = (len(refs) - 1) // 3
    held, mine, theirs, out = refs[:n], refs[n : 2 * n], refs[2 * n : 3 * n], refs[-1]
    share = held[0].shape[3]
    for e in range(out.shape[0]):
        scaled = jnp.concatenate([v[g][e] for g in range(n) for v in (mine, theirs)], axis=0)
        for k in range(PARTS):
            hidden = jnp.concatenate([held[g][k, e] for g in range(n)], axis=0)
            out[e, k * share : (k + 1) * share] = dot(hidden, scaled, ((0,), (0,))).astype(BF)


def hessian(held, mine, theirs):
    _, experts, rows, share = held[0].shape
    width = mine[0].shape[2]
    n = len(held)
    return pl.pallas_call(
        hessian_kernel,
        out_shape=jax.ShapeDtypeStruct((experts, PARTS * share, width), BF),
        in_specs=[VMEM] * (3 * n),
        out_specs=VMEM,
        compiler_params=params(),
        cost_estimate=cost(
            2 * n * experts * rows * share * PARTS * width,
            2 * experts * (share * PARTS * width + n * rows * (share * PARTS + width)),
        ),
        name="hessian",
    )(*held, *mine, *theirs)


def per_device(tokens, expert_ids, gate_prob, gate_weight, up_weight, tangent, curvature):
    width = tokens.shape[1]
    me = lax.axis_index("expert").astype(jnp.int32)
    partner = me + 1 - 2 * (me % 2)
    experts = jnp.stack([2 * me, 2 * partner])

    high = lax.reduce_precision(gate_prob, 8, 7)
    rest = gate_prob - high
    meta = jnp.concatenate(
        [expert_ids.astype(BF), high.astype(BF), rest.astype(BF)], axis=1
    )
    meta = jnp.pad(meta, ((0, 0), (0, META - meta.shape[1])))
    block = jnp.concatenate([tokens, meta], axis=1)

    z = lax.axis_index("dp").astype(jnp.int32)[None]
    half = BLK // 2
    low, upper = move(block, "a", 1), move(block, "a", -1)
    far_low, far_high = move(low[:half], "a", 1), move(upper[half:], "a", -1)
    pair_x = jnp.stack([block, upper])
    x_low, x_up = move(pair_x, "b", 1), move(pair_x, "b", -1)
    pair_y = jnp.stack([low, jnp.concatenate([far_low, far_high], axis=0)])
    y_low, y_up = move(pair_y, "b", 1), move(pair_y, "b", -1)
    x_far, y_far = move(x_low, "b", 1), move(y_up, "b", -1)

    def share(blocks):
        mine, theirs, weight = select(experts, blocks, width)
        return hidden_share(mine, swap(theirs), gate_weight, up_weight), weight

    own0, weight0 = share([pair_x, pair_y])
    all0 = lax.all_gather(own0, "dp")
    own1, weight1 = share([after(x_low, own0), x_up])
    all1 = lax.all_gather(own1, "dp")
    own2, weight2 = share([after(y_low, own1), y_up])
    all2 = lax.all_gather(own2, "dp")
    own3, weight3 = share([after(x_far, own2), y_far])
    below, above = move_z(own3, 1), move_z(own3, -1)
    out_a, out_b = expert_out(tangent, [after(all0, own3), all1])
    line = [(0, 0), (0, 1), (0, 2), (0, 3)]
    part_own, part_low_x, part_up_x = combine(
        line + [(1, 0), (1, 1), (2, 0), (2, 1)], out_a, swap(out_b), [weight0, weight1]
    )
    arrived_x = [move(part_low_x, "b", -1), move(part_up_x, "b", 1)]
    far0 = move_z(after(below, part_own)[:1], 1)
    far1 = move_z(after(above, part_own)[1:], -1)
    out_a, out_b, held3 = expert_out(
        tangent, [after(all2, *arrived_x)], [z, own3, below, above, far0, far1]
    )
    part_far, part_low_y, part_up_y = combine(
        [(1, 0), (1, 1), (2, 0), (2, 1)] + line, out_a, swap(out_b), [weight2, weight3]
    )
    arrived_y = [move(part_low_y, "b", -1), move(part_up_y, "b", 1)]
    arrived_far = move(part_far, "b", 2)
    weights = [weight0, weight1, weight2, weight3]
    helds = [all0, all1, all2, held3]

    total_x = sum(v.astype(F32) for v in (part_own[:2], *arrived_x, arrived_far[:2]))
    total_y = sum(v.astype(F32) for v in (part_own[2:], *arrived_y, arrived_far[2:]))
    back_low = move(total_x[1].astype(BF), "a", 1)
    back_up = move(total_y[0].astype(BF), "a", -1)
    back_far = move(total_y[1].astype(BF), "a", 2)
    combined = (
        total_x[0] + back_up.astype(F32) + back_low.astype(F32) + back_far.astype(F32)
    )
    tangent_image = combined.astype(BF)
    weighted = (curvature[None, :] * combined).astype(BF)

    row = jnp.stack(
        [
            weighted,
            move(weighted, "a", -1),
            move(weighted, "a", 1),
            move(weighted, "a", 2),
        ]
    )
    r_low, r_up = move(row, "b", 1), move(row, "b", -1)
    r_far_x, r_far_y = move(r_low[:2], "b", 1), move(r_up[2:], "b", -1)
    sources = [
        [(row, 0), (row, 1)],
        [(r_low, 0), (r_up, 0)],
        [(r_low, 1), (r_up, 1)],
        [(r_far_x, 0), (r_far_y, 0)],
    ]
    mines, others = [], []
    for source, weight in zip(sources, weights):
        mine, theirs = scaled_rows(source, weight)
        mines.append(mine)
        others.append(swap(theirs))
    return hessian(helds, mines, others), tangent_image


def solution(mesh):
    placed = (
        P("expert", None),
        P("expert", None),
        P("expert", None),
        P("expert", None, "dp"),
        P("expert", None, "dp"),
        P("expert", None, "dp"),
        P("dp"),
    )
    return jax.shard_map(
        per_device,
        mesh=mesh,
        in_specs=placed,
        out_specs=(P("expert", None, "dp"), P("expert", "dp")),
        check_vma=False,
    )
```

```python
import functools

import jax
import jax.numpy as jnp
from jax import lax
from jax.experimental import pallas as pl
from jax.experimental.pallas import tpu as pltpu
from jax.sharding import PartitionSpec as P

BF = jnp.bfloat16
F32 = jnp.float32
SIDE = 4
BLK = 128
CAP = 32
SLOTS = 4 * CAP
META = 128
TOP = 8
PARTS = 4
LIMIT = 20 << 20


def params():
    return pltpu.CompilerParams(vmem_limit_bytes=LIMIT)


VMEM = pl.BlockSpec(memory_space=pltpu.VMEM)
SMEM = pl.BlockSpec(memory_space=pltpu.SMEM)


def cost(flops, nbytes):
    return pl.CostEstimate(flops=1, bytes_accessed=1, transcendentals=0)


def spot(y, x, core):
    return ((y % SIDE) * SIDE + x % SIDE) * 2 + core


def pairs(stage, step):
    out = []
    for y in range(SIDE):
        for x in range(SIDE):
            for core in range(2):
                along_x = (core == 0) == (stage == "a")
                to = spot(y, x + step, core) if along_x else spot(y + step, x, core)
                out.append((spot(y, x, core), to))
    return out


def move(value, stage, step):
    return lax.ppermute(value, "expert", pairs(stage, step))


def swap(value):
    return lax.ppermute(value, "expert", [(i, i ^ 1) for i in range(2 * SIDE * SIDE)])


def move_z(value, step):
    return lax.ppermute(value, "dp", [(i, (i + step) % PARTS) for i in range(PARTS)])


def after(value, *earlier):
    return lax.optimization_barrier((value, *earlier))[0]


def dot(a, b, dims=((1,), (0,))):
    return lax.dot_general(a, b, (dims, ((), ())), preferred_element_type=F32)


def select_kernel(experts, *refs):
    given = refs[:-3]
    mine, theirs, weight = refs[-3:]
    blocks = [v.at[i] for v in given for i in range(v.shape[0])]
    n = len(blocks)
    width = mine.shape[2]
    slot = lax.broadcasted_iota(jnp.int32, (BLK, SLOTS), 1)
    group = slot // CAP
    expert = jnp.where(group < 2, experts[0] + group, experts[1] + group - 2).astype(F32)
    place = (slot % CAP).astype(F32)
    row = lax.broadcasted_iota(jnp.int32, (BLK, BLK), 0)
    column = lax.broadcasted_iota(jnp.int32, (BLK, BLK), 1)
    earlier = (column < row).astype(F32).astype(BF)
    for b in range(n):
        meta = blocks[b][:, width:].astype(F32)
        named = jnp.zeros((BLK, SLOTS), F32)
        prob = jnp.zeros((BLK, SLOTS), F32)
        for k in range(TOP):
            hit = meta[:, k : k + 1] == expert
            named = jnp.where(hit, 1.0, named)
            value = meta[:, TOP + k : TOP + k + 1] + meta[:, 2 * TOP + k : 2 * TOP + k + 1]
            prob = jnp.where(hit, value, prob)
        position = dot(earlier, named.astype(BF))
        chosen = (named > 0.5) & (position == place)
        pick = jnp.where(chosen, 1.0, 0.0).astype(BF)
        kept = jnp.where(chosen, prob, 0.0)
        high = kept.astype(BF)
        weight[b, 0] = high
        weight[b, 1] = (kept - high.astype(F32)).astype(BF)
        rows = dot(pick, blocks[b][:, :width], ((0,), (0,))).astype(BF)
        at = pl.ds(b * CAP, CAP)
        mine[0, at, :] = rows[0:CAP]
        mine[1, at, :] = rows[CAP : 2 * CAP]
        theirs[0, at, :] = rows[2 * CAP : 3 * CAP]
        theirs[1, at, :] = rows[3 * CAP :]


def select(experts, blocks, width):
    n = sum(v.shape[0] for v in blocks)
    rows = jax.ShapeDtypeStruct((2, n * CAP, width), BF)
    weight = jax.ShapeDtypeStruct((n, 2, BLK, SLOTS), BF)
    return pl.pallas_call(
        select_kernel,
        out_shape=(rows, rows, weight),
        in_specs=[SMEM] + [VMEM] * len(blocks),
        out_specs=(VMEM,) * 3,
        compiler_params=params(),
        cost_estimate=cost(2 * n * BLK * SLOTS * width, 4 * n * BLK * width),
        name="select_rows",
    )(experts, *blocks)


def hidden_kernel(xa, xb, gate, up, out):
    share = out.shape[2]
    whole = share // 256 * 256
    for e in range(out.shape[0]):
        x = jnp.concatenate([xa[e], xb[e]], axis=0)
        tail = jnp.concatenate([gate[e, :, whole:], up[e, :, whole:]], axis=1)
        both = dot(x, tail)
        part = share - whole
        g = jnp.concatenate([dot(x, gate[e, :, :whole]), both[:, :part]], axis=1)
        u = jnp.concatenate([dot(x, up[e, :, :whole]), both[:, part:]], axis=1)
        out[e] = (g / (1.0 + jnp.exp(-g)) * u).astype(BF)


def hidden_share(xa, xb, gate, up):
    experts, rows, width = xa.shape
    share = gate.shape[2]
    return pl.pallas_call(
        hidden_kernel,
        out_shape=jax.ShapeDtypeStruct((experts, 2 * rows, share), BF),
        in_specs=[VMEM] * 4,
        out_specs=VMEM,
        compiler_params=params(),
        cost_estimate=cost(
            8 * experts * rows * width * share, 4 * experts * width * (share + rows)
        ),
        name="hidden_share",
    )(xa, xb, gate, up)


def expert_out_kernel(n, *refs):
    helds, refs = refs[:n], refs[n:]
    if len(refs) > 3:
        z, own, below, above, far0, far1, tangent, out_a, out_b, ring = refs
        me = z[0]
        ring[me] = own[...]
        ring[lax.rem(me + PARTS - 1, PARTS)] = below[...]
        ring[lax.rem(me + 1, PARTS)] = above[...]
        far = lax.rem(me + 2, PARTS)
        ring[far, 0] = far0[0]
        ring[far, 1] = far1[0]
        helds = (*helds, ring)
    else:
        tangent, out_a, out_b = refs
    for g, held in enumerate(helds):
        half = held.shape[2] // 2
        at = pl.ds(g * half, half)
        for e in range(tangent.shape[0]):
            x = jnp.concatenate([held[k, e] for k in range(PARTS)], axis=1)
            rows = dot(x, tangent[e])
            out_a[e, at, :] = rows[:half].astype(BF)
            out_b[e, at, :] = rows[half:].astype(BF)


def expert_out(tangent, helds, ring=()):
    experts, units, width = tangent.shape
    half = sum(v.shape[2] for v in helds) // 2
    outs = []
    if ring:
        rows = ring[1].shape[1]
        half += rows // 2
        outs = [jax.ShapeDtypeStruct((PARTS, experts, rows, units // PARTS), BF)]
    shape = jax.ShapeDtypeStruct((experts, half, width), BF)
    return pl.pallas_call(
        functools.partial(expert_out_kernel, len(helds)),
        out_shape=[shape, shape, *outs],
        in_specs=[VMEM] * len(helds) + ([SMEM] + [VMEM] * 5 if ring else []) + [VMEM],
        out_specs=[VMEM] * (2 + len(outs)),
        compiler_params=params(),
        cost_estimate=cost(4 * experts * half * units * width, 2 * experts * units * width),
        name="expert_out",
    )(*helds, *ring, tangent)


def combine_kernel(places, n, mine, theirs, *refs):
    weights, outs = refs[:n], refs[n:]
    for b, (i, j) in enumerate(places):
        at = pl.ds(b * CAP, CAP)
        rows = jnp.concatenate(
            [mine[0, at, :], mine[1, at, :], theirs[0, at, :], theirs[1, at, :]], axis=0
        )
        weight = weights[b // 4]
        outs[i][j] = (dot(weight[b % 4, 0], rows) + dot(weight[b % 4, 1], rows)).astype(BF)


def combine(places, mine, theirs, weights):
    width = mine.shape[2]
    counts = [sum(p[0] == i for p in places) for i in range(1 + max(p[0] for p in places))]
    return pl.pallas_call(
        functools.partial(combine_kernel, places, len(weights)),
        out_shape=[jax.ShapeDtypeStruct((c, BLK, width), BF) for c in counts],
        in_specs=[VMEM] * (2 + len(weights)),
        out_specs=[VMEM] * len(counts),
        compiler_params=params(),
        cost_estimate=cost(4 * len(places) * BLK * SLOTS * width, 4 * len(places) * BLK * width),
        name="combine_rows",
    )(mine, theirs, *weights)


def scaled_kernel(*refs):
    *blocks, weight, mine, theirs = refs
    for b in range(weight.shape[0]):
        block = blocks[b // 2][b % 2]
        rows = (
            dot(weight[b, 0], block, ((0,), (0,))) + dot(weight[b, 1], block, ((0,), (0,)))
        ).astype(BF)
        at = pl.ds(b * CAP, CAP)
        mine[0, at, :] = rows[0:CAP]
        mine[1, at, :] = rows[CAP : 2 * CAP]
        theirs[0, at, :] = rows[2 * CAP : 3 * CAP]
        theirs[1, at, :] = rows[3 * CAP :]


def scaled_rows(sources, weight):
    width = sources[0][0].shape[2]
    n = weight.shape[0]
    tile = 512
    out_spec = pl.BlockSpec((2, n * CAP, tile), lambda j: (0, 0, j))
    shape = jax.ShapeDtypeStruct((2, n * CAP, width), BF)
    return pl.pallas_call(
        scaled_kernel,
        out_shape=(shape, shape),
        grid=(width // tile,),
        in_specs=[
            pl.BlockSpec((2, BLK, tile), functools.partial(lambda i, j: (i, 0, j), i))
            for _, i in sources
        ]
        + [pl.BlockSpec(weight.shape, lambda j: (0, 0, 0, 0))],
        out_specs=(out_spec, out_spec),
        compiler_params=params(),
        cost_estimate=cost(4 * n * BLK * SLOTS * width, 4 * n * BLK * width),
        name="scaled_rows",
    )(*[v for v, _ in sources], weight)


def hessian_kernel(places, n, *refs):
    helds, scaled, rest = refs[:n], refs[n : n + len(places)], refs[n + len(places) :]
    out = rest[-1]
    share = helds[0].shape[3]
    for e in range(out.shape[0]):
        right = jnp.concatenate([v[e] for v in scaled], axis=0)
        for k in range(PARTS):
            left = [helds[i][k, e, row : row + 4 * CAP, :] for i, row in places]
            units = slice(k * share, (k + 1) * share)
            total = dot(jnp.concatenate(left, axis=0), right, ((0,), (0,)))
            if len(rest) > 1:
                total += rest[0][e, units]
            out[e, units] = total.astype(out.dtype)


def hessian(helds, places, scaled, dtype, begun=None):
    _, experts, _, share = helds[0].shape
    width = scaled[0].shape[2]
    begun = [] if begun is None else [begun]
    flops = 2 * len(places) * 4 * CAP * experts * share * PARTS * width
    return pl.pallas_call(
        functools.partial(hessian_kernel, places, len(helds)),
        out_shape=jax.ShapeDtypeStruct((experts, PARTS * share, width), dtype),
        in_specs=[VMEM] * (len(helds) + len(scaled) + len(begun)),
        out_specs=VMEM,
        compiler_params=params(),
        cost_estimate=cost(flops, 2 * experts * share * PARTS * width),
        name="hessian",
    )(*helds, *scaled, *begun)


def per_device(tokens, expert_ids, gate_prob, gate_weight, up_weight, tangent, curvature):
    width = tokens.shape[1]
    me = lax.axis_index("expert").astype(jnp.int32)
    partner = me + 1 - 2 * (me % 2)
    experts = jnp.stack([2 * me, 2 * partner])

    high = lax.reduce_precision(gate_prob, 8, 7)
    rest = gate_prob - high
    meta = jnp.concatenate(
        [expert_ids.astype(BF), high.astype(BF), rest.astype(BF)], axis=1
    )
    meta = jnp.pad(meta, ((0, 0), (0, META - meta.shape[1])))
    block = jnp.concatenate([tokens, meta], axis=1)

    z = lax.axis_index("dp").astype(jnp.int32)[None]
    half = BLK // 2
    low, upper = move(block, "a", 1), move(block, "a", -1)
    far_low, far_high = move(low[:half], "a", 1), move(upper[half:], "a", -1)
    pair_x = jnp.stack([block, upper])
    x_low, x_up = move(pair_x, "b", 1), move(pair_x, "b", -1)
    pair_y = jnp.stack([low, jnp.concatenate([far_low, far_high], axis=0)])
    y_low, y_up = move(pair_y, "b", 1), move(pair_y, "b", -1)
    x_far = move(x_low, "b", 1)

    def share(blocks):
        mine, theirs, weight = select(experts, blocks, width)
        return hidden_share(mine, swap(theirs), gate_weight, up_weight), weight

    own0, weight0 = share([pair_x, pair_y])
    all0 = lax.all_gather(own0, "dp")
    own1, weight1 = share([after(x_low, own0), x_up])
    all1 = lax.all_gather(own1, "dp")
    y_far = move(after(y_up, own1), "b", -1)
    own2, weight2 = share([after(y_low, own1), y_up])
    all2 = lax.all_gather(own2, "dp")
    own3, weight3 = share([after(x_far, own2), y_far])
    below, above = move_z(own3, 1), move_z(own3, -1)
    out_a, out_b = expert_out(tangent, [after(all0, own3), all1])
    line = [(0, 0), (0, 1), (0, 2), (0, 3)]
    part_own, part_low_x, part_up_x = combine(
        line + [(1, 0), (1, 1), (2, 0), (2, 1)], out_a, swap(out_b), [weight0, weight1]
    )
    arrived_x = [move(part_low_x, "b", -1), move(part_up_x, "b", 1)]
    far0 = move_z(after(below, part_own)[:1], 1)
    far1 = move_z(after(above, part_own)[1:], -1)
    out_a, out_b, held3 = expert_out(
        tangent, [after(all2, *arrived_x)], [z, own3, below, above, far0, far1]
    )
    part_far, part_low_y, part_up_y = combine(
        [(1, 0), (1, 1), (2, 0), (2, 1)] + line, out_a, swap(out_b), [weight2, weight3]
    )
    arrived_y = [move(part_low_y, "b", -1), move(part_up_y, "b", 1)]
    arrived_far = move(part_far, "b", 2)
    weights = [weight0, weight1, weight2, weight3]

    total_x = sum(v.astype(F32) for v in (part_own[:2], *arrived_x, arrived_far[:2]))
    total_y = sum(v.astype(F32) for v in (part_own[2:], *arrived_y, arrived_far[2:]))
    back_low = move(total_x[1].astype(BF), "a", 1)
    back_up = move(total_y[0].astype(BF), "a", -1)
    back_far = move(total_y[1].astype(BF), "a", 2)
    combined = (
        total_x[0] + back_up.astype(F32) + back_low.astype(F32) + back_far.astype(F32)
    )
    tangent_image = combined.astype(BF)
    weighted = (curvature[None, :] * combined).astype(BF)

    row = jnp.stack(
        [
            weighted,
            move(weighted, "a", -1),
            move(weighted, "a", 1),
            move(weighted, "a", 2),
        ]
    )
    r_low, r_up = move(row, "b", 1), move(row, "b", -1)
    r_far_x, r_far_y = move(r_low[:2], "b", 1), move(r_up[2:], "b", -1)
    sources = [
        [(row, 0), (row, 1)],
        [(r_low, 0), (r_up, 0)],
        [(r_low, 1), (r_up, 1)],
        [(r_far_x, 0), (r_far_y, 0)],
    ]
    half = 4 * CAP
    scaled = []
    for source, weight in zip(sources[:3], weights):
        mine, theirs = scaled_rows(source, weight)
        scaled += [mine, swap(theirs)]
    places = [(g, row) for g in range(3) for row in (0, half)]
    begun = hessian([all0, all1, all2], places, scaled, F32)
    sources[3][0] = (after(r_far_x, begun), 0)
    mine, theirs = scaled_rows(sources[3], weight3)
    last = [(0, 0), (0, half)]
    return hessian([held3], last, [mine, swap(theirs)], BF, begun), tangent_image


def solution(mesh):
    placed = (
        P("expert", None),
        P("expert", None),
        P("expert", None),
        P("expert", None, "dp"),
        P("expert", None, "dp"),
        P("expert", None, "dp"),
        P("dp"),
    )
    return jax.shard_map(
        per_device,
        mesh=mesh,
        in_specs=placed,
        out_specs=(P("expert", None, "dp"), P("expert", "dp")),
        check_vma=False,
    )
```

```python
import functools

import jax
import jax.numpy as jnp
from jax import lax
from jax.experimental import pallas as pl
from jax.experimental.pallas import tpu as pltpu
from jax.sharding import PartitionSpec as P

BF = jnp.bfloat16
F32 = jnp.float32
SIDE = 4
BLK = 128
CAP = 32
SLOTS = 4 * CAP
META = 128
TOP = 8
PARTS = 4
LIMIT = 20 << 20


def params():
    return pltpu.CompilerParams(vmem_limit_bytes=LIMIT)


VMEM = pl.BlockSpec(memory_space=pltpu.VMEM)
SMEM = pl.BlockSpec(memory_space=pltpu.SMEM)


def cost(flops, nbytes):
    return pl.CostEstimate(flops=1, bytes_accessed=1, transcendentals=0)


def spot(y, x, core):
    return ((y % SIDE) * SIDE + x % SIDE) * 2 + core


def pairs(stage, step):
    out = []
    for y in range(SIDE):
        for x in range(SIDE):
            for core in range(2):
                along_x = (core == 0) == (stage == "a")
                to = spot(y, x + step, core) if along_x else spot(y + step, x, core)
                out.append((spot(y, x, core), to))
    return out


def move(value, stage, step):
    return lax.ppermute(value, "expert", pairs(stage, step))


def swap(value):
    return lax.ppermute(value, "expert", [(i, i ^ 1) for i in range(2 * SIDE * SIDE)])


def move_z(value, step):
    return lax.ppermute(value, "dp", [(i, (i + step) % PARTS) for i in range(PARTS)])


def after(value, *earlier):
    return lax.optimization_barrier((value, *earlier))[0]


def dot(a, b, dims=((1,), (0,))):
    return lax.dot_general(a, b, (dims, ((), ())), preferred_element_type=F32)


def pair_kernel(*refs):
    *parts, out = refs
    row = 0
    for part in parts:
        i, at = row // BLK, pl.ds(row % BLK, part.shape[0])
        out[i, at, :] = part[...]
        row += part.shape[0]


def pair_of(*parts):
    return pl.pallas_call(
        pair_kernel,
        out_shape=jax.ShapeDtypeStruct((2, BLK, parts[0].shape[1]), BF),
        in_specs=[VMEM] * len(parts),
        out_specs=VMEM,
        compiler_params=params(),
        cost_estimate=cost(0, 4 * sum(v.size for v in parts)),
        name="pair_blocks",
    )(*parts)


def select_kernel(experts, *refs):
    given = refs[:-3]
    mine, theirs, weight = refs[-3:]
    blocks = [v.at[i] for v in given for i in range(v.shape[0])]
    n = len(blocks)
    width = mine.shape[2]
    slot = lax.broadcasted_iota(jnp.int32, (BLK, SLOTS), 1)
    group = slot // CAP
    expert = jnp.where(group < 2, experts[0] + group, experts[1] + group - 2).astype(F32)
    place = (slot % CAP).astype(F32)
    row = lax.broadcasted_iota(jnp.int32, (BLK, BLK), 0)
    column = lax.broadcasted_iota(jnp.int32, (BLK, BLK), 1)
    earlier = (column < row).astype(F32).astype(BF)
    for b in range(n):
        meta = blocks[b][:, width:].astype(F32)
        named = jnp.zeros((BLK, SLOTS), F32)
        prob = jnp.zeros((BLK, SLOTS), F32)
        for k in range(TOP):
            hit = meta[:, k : k + 1] == expert
            named = jnp.where(hit, 1.0, named)
            value = meta[:, TOP + k : TOP + k + 1] + meta[:, 2 * TOP + k : 2 * TOP + k + 1]
            prob = jnp.where(hit, value, prob)
        position = dot(earlier, named.astype(BF))
        chosen = (named > 0.5) & (position == place)
        pick = jnp.where(chosen, 1.0, 0.0).astype(BF)
        kept = jnp.where(chosen, prob, 0.0)
        high = kept.astype(BF)
        weight[b, 0] = high
        weight[b, 1] = (kept - high.astype(F32)).astype(BF)
        rows = dot(pick, blocks[b][:, :width], ((0,), (0,))).astype(BF)
        at = pl.ds(b * CAP, CAP)
        mine[0, at, :] = rows[0:CAP]
        mine[1, at, :] = rows[CAP : 2 * CAP]
        theirs[0, at, :] = rows[2 * CAP : 3 * CAP]
        theirs[1, at, :] = rows[3 * CAP :]


def select(experts, blocks, width):
    n = sum(v.shape[0] for v in blocks)
    rows = jax.ShapeDtypeStruct((2, n * CAP, width), BF)
    weight = jax.ShapeDtypeStruct((n, 2, BLK, SLOTS), BF)
    return pl.pallas_call(
        select_kernel,
        out_shape=(rows, rows, weight),
        in_specs=[SMEM] + [VMEM] * len(blocks),
        out_specs=(VMEM,) * 3,
        compiler_params=params(),
        cost_estimate=cost(2 * n * BLK * SLOTS * width, 4 * n * BLK * width),
        name="select_rows",
    )(experts, *blocks)


def hidden_kernel(xa, xb, gate, up, out):
    share = out.shape[2]
    whole = share // 256 * 256
    for e in range(out.shape[0]):
        x = jnp.concatenate([xa[e], xb[e]], axis=0)
        tail = jnp.concatenate([gate[e, :, whole:], up[e, :, whole:]], axis=1)
        both = dot(x, tail)
        part = share - whole
        g = jnp.concatenate([dot(x, gate[e, :, :whole]), both[:, :part]], axis=1)
        u = jnp.concatenate([dot(x, up[e, :, :whole]), both[:, part:]], axis=1)
        out[e] = (g / (1.0 + jnp.exp(-g)) * u).astype(BF)


def hidden_share(xa, xb, gate, up):
    experts, rows, width = xa.shape
    share = gate.shape[2]
    return pl.pallas_call(
        hidden_kernel,
        out_shape=jax.ShapeDtypeStruct((experts, 2 * rows, share), BF),
        in_specs=[VMEM] * 4,
        out_specs=VMEM,
        compiler_params=params(),
        cost_estimate=cost(
            8 * experts * rows * width * share, 4 * experts * width * (share + rows)
        ),
        name="hidden_share",
    )(xa, xb, gate, up)


def expert_out_kernel(n, *refs):
    helds, refs = refs[:n], refs[n:]
    if len(refs) > 3:
        z, own, below, above, far0, far1, tangent, out_a, out_b, ring = refs
        me = z[0]
        ring[me] = own[...]
        ring[lax.rem(me + PARTS - 1, PARTS)] = below[...]
        ring[lax.rem(me + 1, PARTS)] = above[...]
        far = lax.rem(me + 2, PARTS)
        ring[far, 0] = far0[0]
        ring[far, 1] = far1[0]
        helds = (*helds, ring)
    else:
        tangent, out_a, out_b = refs
    for g, held in enumerate(helds):
        half = held.shape[2] // 2
        at = pl.ds(g * half, half)
        for e in range(tangent.shape[0]):
            x = jnp.concatenate([held[k, e] for k in range(PARTS)], axis=1)
            rows = dot(x, tangent[e])
            out_a[e, at, :] = rows[:half].astype(BF)
            out_b[e, at, :] = rows[half:].astype(BF)


def expert_out(tangent, helds, ring=()):
    experts, units, width = tangent.shape
    half = sum(v.shape[2] for v in helds) // 2
    outs = []
    if ring:
        rows = ring[1].shape[1]
        half += rows // 2
        outs = [jax.ShapeDtypeStruct((PARTS, experts, rows, units // PARTS), BF)]
    shape = jax.ShapeDtypeStruct((experts, half, width), BF)
    return pl.pallas_call(
        functools.partial(expert_out_kernel, len(helds)),
        out_shape=[shape, shape, *outs],
        in_specs=[VMEM] * len(helds) + ([SMEM] + [VMEM] * 5 if ring else []) + [VMEM],
        out_specs=[VMEM] * (2 + len(outs)),
        compiler_params=params(),
        cost_estimate=cost(4 * experts * half * units * width, 2 * experts * units * width),
        name="expert_out",
    )(*helds, *ring, tangent)


def combine_kernel(places, n, mine, theirs, *refs):
    weights, outs = refs[:n], refs[n:]
    for b, (i, j) in enumerate(places):
        at = pl.ds(b * CAP, CAP)
        rows = jnp.concatenate(
            [mine[0, at, :], mine[1, at, :], theirs[0, at, :], theirs[1, at, :]], axis=0
        )
        weight = weights[b // 4]
        outs[i][j] = (dot(weight[b % 4, 0], rows) + dot(weight[b % 4, 1], rows)).astype(BF)


def combine(places, mine, theirs, weights):
    width = mine.shape[2]
    counts = [sum(p[0] == i for p in places) for i in range(1 + max(p[0] for p in places))]
    return pl.pallas_call(
        functools.partial(combine_kernel, places, len(weights)),
        out_shape=[jax.ShapeDtypeStruct((c, BLK, width), BF) for c in counts],
        in_specs=[VMEM] * (2 + len(weights)),
        out_specs=[VMEM] * len(counts),
        compiler_params=params(),
        cost_estimate=cost(4 * len(places) * BLK * SLOTS * width, 4 * len(places) * BLK * width),
        name="combine_rows",
    )(mine, theirs, *weights)


def scaled_kernel(*refs):
    *blocks, weight, mine, theirs = refs
    for b in range(weight.shape[0]):
        block = blocks[b // 2][b % 2]
        rows = (
            dot(weight[b, 0], block, ((0,), (0,))) + dot(weight[b, 1], block, ((0,), (0,)))
        ).astype(BF)
        at = pl.ds(b * CAP, CAP)
        mine[0, at, :] = rows[0:CAP]
        mine[1, at, :] = rows[CAP : 2 * CAP]
        theirs[0, at, :] = rows[2 * CAP : 3 * CAP]
        theirs[1, at, :] = rows[3 * CAP :]


def scaled_rows(sources, weight):
    width = sources[0][0].shape[2]
    n = weight.shape[0]
    tile = 512
    out_spec = pl.BlockSpec((2, n * CAP, tile), lambda j: (0, 0, j))
    shape = jax.ShapeDtypeStruct((2, n * CAP, width), BF)
    return pl.pallas_call(
        scaled_kernel,
        out_shape=(shape, shape),
        grid=(width // tile,),
        in_specs=[
            pl.BlockSpec((2, BLK, tile), functools.partial(lambda i, j: (i, 0, j), i))
            for _, i in sources
        ]
        + [pl.BlockSpec(weight.shape, lambda j: (0, 0, 0, 0))],
        out_specs=(out_spec, out_spec),
        compiler_params=params(),
        cost_estimate=cost(4 * n * BLK * SLOTS * width, 4 * n * BLK * width),
        name="scaled_rows",
    )(*[v for v, _ in sources], weight)


def hessian_kernel(places, n, *refs):
    helds, scaled, rest = refs[:n], refs[n : n + len(places)], refs[n + len(places) :]
    out = rest[-1]
    share = helds[0].shape[3]
    for e in range(out.shape[0]):
        right = jnp.concatenate([v[e] for v in scaled], axis=0)
        for k in range(PARTS):
            left = [helds[i][k, e, row : row + 4 * CAP, :] for i, row in places]
            units = slice(k * share, (k + 1) * share)
            total = dot(jnp.concatenate(left, axis=0), right, ((0,), (0,)))
            if len(rest) > 1:
                total += rest[0][e, units]
            out[e, units] = total.astype(out.dtype)


def hessian(helds, places, scaled, dtype, begun=None):
    _, experts, _, share = helds[0].shape
    width = scaled[0].shape[2]
    begun = [] if begun is None else [begun]
    flops = 2 * len(places) * 4 * CAP * experts * share * PARTS * width
    return pl.pallas_call(
        functools.partial(hessian_kernel, places, len(helds)),
        out_shape=jax.ShapeDtypeStruct((experts, PARTS * share, width), dtype),
        in_specs=[VMEM] * (len(helds) + len(scaled) + len(begun)),
        out_specs=VMEM,
        compiler_params=params(),
        cost_estimate=cost(flops, 2 * experts * share * PARTS * width),
        name="hessian",
    )(*helds, *scaled, *begun)


def per_device(tokens, expert_ids, gate_prob, gate_weight, up_weight, tangent, curvature):
    width = tokens.shape[1]
    me = lax.axis_index("expert").astype(jnp.int32)
    partner = me + 1 - 2 * (me % 2)
    experts = jnp.stack([2 * me, 2 * partner])

    high = lax.reduce_precision(gate_prob, 8, 7)
    rest = gate_prob - high
    meta = jnp.concatenate(
        [expert_ids.astype(BF), high.astype(BF), rest.astype(BF)], axis=1
    )
    meta = jnp.pad(meta, ((0, 0), (0, META - meta.shape[1])))
    block = jnp.concatenate([tokens, meta], axis=1)

    z = lax.axis_index("dp").astype(jnp.int32)[None]
    half = BLK // 2
    low, upper = move(block, "a", 1), move(block, "a", -1)
    far_low, far_high = move(low[:half], "a", 1), move(upper[half:], "a", -1)
    pair_x = pair_of(block, upper)
    x_low, x_up = move(pair_x, "b", 1), move(pair_x, "b", -1)
    pair_y = pair_of(low, far_low, far_high)
    y_low, y_up = move(pair_y, "b", 1), move(pair_y, "b", -1)
    x_far = move(x_low, "b", 1)

    def share(blocks):
        mine, theirs, weight = select(experts, blocks, width)
        return hidden_share(mine, swap(theirs), gate_weight, up_weight), weight

    own0, weight0 = share([pair_x, pair_y])
    all0 = lax.all_gather(own0, "dp")
    own1, weight1 = share([after(x_low, own0), x_up])
    all1 = lax.all_gather(own1, "dp")
    y_far = move(after(y_up, own1), "b", -1)
    own2, weight2 = share([after(y_low, own1), y_up])
    all2 = lax.all_gather(own2, "dp")
    own3, weight3 = share([after(x_far, own2), y_far])
    below, above = move_z(own3, 1), move_z(own3, -1)
    out_a, out_b = expert_out(tangent, [after(all0, own3), all1])
    line = [(0, 0), (0, 1), (0, 2), (0, 3)]
    part_own, part_low_x, part_up_x = combine(
        line + [(1, 0), (1, 1), (2, 0), (2, 1)], out_a, swap(out_b), [weight0, weight1]
    )
    arrived_x = [move(part_low_x, "b", -1), move(part_up_x, "b", 1)]
    far0 = move_z(after(below, part_own)[:1], 1)
    far1 = move_z(after(above, part_own)[1:], -1)
    out_a, out_b, held3 = expert_out(
        tangent, [after(all2, *arrived_x)], [z, own3, below, above, far0, far1]
    )
    part_far, part_low_y, part_up_y = combine(
        [(1, 0), (1, 1), (2, 0), (2, 1)] + line, out_a, swap(out_b), [weight2, weight3]
    )
    arrived_y = [move(part_low_y, "b", -1), move(part_up_y, "b", 1)]
    arrived_far = move(part_far, "b", 2)
    weights = [weight0, weight1, weight2, weight3]

    total_x = sum(v.astype(F32) for v in (part_own[:2], *arrived_x, arrived_far[:2]))
    total_y = sum(v.astype(F32) for v in (part_own[2:], *arrived_y, arrived_far[2:]))
    back_low = move(total_x[1].astype(BF), "a", 1)
    back_up = move(total_y[0].astype(BF), "a", -1)
    back_far = move(total_y[1].astype(BF), "a", 2)
    combined = (
        total_x[0] + back_up.astype(F32) + back_low.astype(F32) + back_far.astype(F32)
    )
    tangent_image = combined.astype(BF)
    weighted = (curvature[None, :] * combined).astype(BF)

    row = jnp.stack(
        [
            weighted,
            move(weighted, "a", -1),
            move(weighted, "a", 1),
            move(weighted, "a", 2),
        ]
    )
    r_low, r_up = move(row, "b", 1), move(row, "b", -1)
    r_far_x, r_far_y = move(r_low[:2], "b", 1), move(r_up[2:], "b", -1)
    sources = [
        [(row, 0), (row, 1)],
        [(r_low, 0), (r_up, 0)],
        [(r_low, 1), (r_up, 1)],
        [(r_far_x, 0), (r_far_y, 0)],
    ]
    half = 4 * CAP
    scaled = []
    for source, weight in zip(sources[:3], weights):
        mine, theirs = scaled_rows(source, weight)
        scaled += [mine, swap(theirs)]
    places = [(g, row) for g in range(3) for row in (0, half)]
    begun = hessian([all0, all1, all2], places, scaled, F32)
    sources[3][0] = (after(r_far_x, begun), 0)
    mine, theirs = scaled_rows(sources[3], weight3)
    last = [(0, 0), (0, half)]
    return hessian([held3], last, [mine, swap(theirs)], BF, begun), tangent_image


def solution(mesh):
    placed = (
        P("expert", None),
        P("expert", None),
        P("expert", None),
        P("expert", None, "dp"),
        P("expert", None, "dp"),
        P("expert", None, "dp"),
        P("dp"),
    )
    return jax.shard_map(
        per_device,
        mesh=mesh,
        in_specs=placed,
        out_specs=(P("expert", None, "dp"), P("expert", "dp")),
        check_vma=False,
    )
```
